512 devices in a mesh: ch: 8 (over x, z_hi), ctx: 64 (over y, z_lo, core).
Axes of the slice: x: 4, y: 4, z: 16 (z_hi: 2, z_lo: 8; z = z_hi * 8 + z_lo), core: 2. Of those that a mesh axis runs over, the one named last changes fastest.
Arguments:
- signal: bfloat16 [16384, 8192], P('ctx', 'ch'), may hold values from -6 to 6
- gate: bfloat16 [16384, 8192], P('ctx', 'ch'), may hold values from -6 to 6
- filter_taps: bfloat16 [16384, 8192], P('ctx', 'ch'), may hold values from -0.21875 to 0.21875
- skip: bfloat16 [8192], P('ch'), may hold values from -4 to 4
- residual: bfloat16 [16384, 8192], P('ctx', 'ch'), may hold values from -70 to 70
- gain: bfloat16 [8192], P('ch'), may hold values from 0.5 to 1.5
Outputs:
- new_residual: bfloat16 [16384, 8192], P('ctx', 'ch')
- normed: bfloat16 [16384, 8192], P('ctx', 'ch')
The draws below stay inside these ranges and needn't reach their ends.
All inputs are finite; a program needn't handle non-finite values.
Results may differ from the reference program's by a relative error of at most 0.0075.
Values may be sent and summed in bfloat16 or wider, within the bound.
No kernel may reach another device: no remote copies, remote signals or barrier semaphores. Data moves between devices by JAX's collectives and lax.ppermute only.
A program may use at most 64 MiB of HBM per device.

```python
import math
import jax
import jax.numpy as jnp
from jax import lax

D = 8192
BLOCK = 256
PANELS = 3
TOKENS = 16384


def draw_residual(key, part):
    key = jax.random.fold_in(key, 11)
    first, second, third = jax.random.split(key, 3)
    columns = jnp.arange(D, dtype=jnp.float32)
    rising = jnp.sqrt(1.0 + 2.0 * columns / D)
    column_scale = 10.0 ** (jax.random.uniform(second, (D,), dtype=jnp.float32) - 0.5)
    row_scale = 10.0 ** (jax.random.uniform(third, (TOKENS,), dtype=jnp.float32) - 0.5)
    base = jnp.clip(jax.random.normal(first, (TOKENS, D), dtype=jnp.float32), -4.0, 4.0)
    values = base * row_scale[:, None] * (column_scale * rising)[None, :]
    return values.astype(jnp.bfloat16)


def block_scale(key, dims, cuts, smallest, high):
    def one(dim, blocks):
        steps = jax.random.uniform(jax.random.fold_in(jax.random.fold_in(key, 6), dim), (blocks,), jnp.float32, smallest / len(cuts), high / len(cuts))
        return jnp.repeat(jnp.exp(steps), dims[dim] // blocks).reshape((-1,) + (1,) * (len(dims) - dim - 1))

    factor_of = one(*cuts[0])
    for cut in cuts[1:]:
        factor_of = factor_of * one(*cut)
    return factor_of


def noise(key, shape, scale, most, cuts=(), held_as=jnp.bfloat16):
    values = jax.random.normal(key, shape, jnp.float32) * scale
    if len(cuts) > 0:
        values = block_scale(key, shape, cuts, -0.22, 0.18) * values
    return jnp.clip(values, min=-most, max=most).astype(held_as)


def setup_inputs(seed: int = 0) -> dict:
    seeds = jax.random.split(jax.random.key(seed), 7)
    signal = noise(seeds[0], (TOKENS, D), 1.0, 6.0, ((0, 64), (1, 8)))
    gate = noise(seeds[1], (TOKENS, D), 1.0, 6.0, ((0, 64), (1, 8)))
    filter_taps = noise(seeds[2], (TOKENS, D), (PANELS * BLOCK) ** -0.5, 0.21875, ((0, 64), (1, 8)))
    skip = noise(seeds[3], (D,), 1.0, 4.0, ((0, 8),))
    residual = draw_residual(jax.random.fold_in(seeds[6], 71), 0)
    gain = jnp.clip(1.0 + 0.1 * jax.random.normal(seeds[5], (D,), jnp.float32), 0.5, 1.5).astype(jnp.bfloat16)
    return dict(signal=signal, gate=gate, filter_taps=filter_taps, skip=skip, residual=residual, gain=gain)


def reference(signal, gate, filter_taps, skip, residual, gain):
    kept_lags = PANELS * BLOCK
    group = math.gcd(D, 512)
    count = D // group

    def convolve(pair):
        block_signal, block_taps = pair
        lags = jnp.arange(TOKENS, dtype=jnp.int32)[:, None]
        kept = jnp.where(lags < kept_lags, block_taps.astype(jnp.float32), jnp.zeros_like(block_taps, dtype=jnp.float32))
        product = jnp.fft.rfft(block_signal.astype(jnp.float32), axis=0) * jnp.fft.rfft(kept, axis=0)
        return jnp.fft.irfft(product, n=TOKENS, axis=0).astype(jnp.float32)
    grouped_signal = signal.reshape(TOKENS, count, group).transpose(1, 0, 2)
    grouped_taps = filter_taps.reshape(TOKENS, count, group).transpose(1, 0, 2)
    conv = lax.map(convolve, (grouped_signal, grouped_taps)).transpose(1, 0, 2).reshape(TOKENS, D)
    mixed = gate.astype(jnp.float32) * (conv + skip.astype(jnp.float32)[None, :] * signal.astype(jnp.float32))
    new_residual = (residual.astype(jnp.float32) + mixed).astype(jnp.bfloat16)
    widened = lax.optimization_barrier(new_residual).astype(jnp.float32)
    mean_square = lax.optimization_barrier(jnp.mean(widened * widened, axis=1, keepdims=True))
    normed = (widened * lax.rsqrt(mean_square + 1e-05) * gain.astype(jnp.float32)[None, :]).astype(jnp.bfloat16)
    return (new_residual, normed)
```

```python
import functools
import math

import jax
import jax.numpy as jnp
import ml_dtypes
import numpy as np
from jax import lax
from jax.experimental import pallas as pl
from jax.experimental.pallas import tpu as pltpu
from jax.sharding import PartitionSpec as P

D = 8192
BLOCK = 256
PANELS = 3
HALF = 512
QUARTER = 128
LAGS = PANELS * BLOCK
WINDOW = LAGS + 2 * BLOCK
BINS = WINDOW // 2
TILE = 128
EPS = 1e-05
Y, Z, CORES = 4, 8, 2


def split(values):
    high = values.astype(np.float32).astype(ml_dtypes.bfloat16)
    low = (values - high.astype(np.float64)).astype(np.float32).astype(ml_dtypes.bfloat16)
    return high, low


@functools.cache
def tables():
    bins = np.arange(BINS)[:, None]
    points = np.arange(WINDOW)[None, :]
    angle = (bins * points % WINDOW) * (2 * math.pi / WINDOW)
    sign = (1.0 - 2.0 * (points % 2))[0]
    real = np.cos(angle)
    imag = -np.sin(angle)
    imag[0] = sign
    forward = np.concatenate([real, imag], axis=0)
    scale = np.where(np.arange(BINS) == 0, 1.0, 2.0)[:, None] / WINDOW
    back = np.concatenate([real * scale, imag * scale], axis=0).T[LAGS:]
    return split(forward), split(back)


def pairs(rule):
    result = []
    for index in range(Y * Z * CORES):
        target = rule(index // (Z * CORES), index // CORES % Z, index % CORES)
        if target is not None:
            y, z, core = target
            result.append((index, y % Y * Z * CORES + z * CORES + core))
    return result


def move(x, rule):
    return lax.ppermute(x, "ctx", pairs(rule))


def dot(a, b):
    return jnp.dot(a, b, preferred_element_type=jnp.float32)


def spectrum_kernel(high, low, x, out):
    for tile in range(WINDOW // BLOCK):
        rows = slice(tile * BLOCK, (tile + 1) * BLOCK)
        out[rows, :] = dot(high[rows, :], x[...]) + dot(low[rows, :], x[...])


def spectrum(high, low, x):
    return pl.pallas_call(
        spectrum_kernel,
        out_shape=jax.ShapeDtypeStruct((WINDOW, HALF), jnp.float32),
        in_specs=[pl.BlockSpec(memory_space=pltpu.VMEM)] * 3,
        out_specs=pl.BlockSpec(memory_space=pltpu.VMEM),
        compiler_params=pltpu.CompilerParams(vmem_limit_bytes=24 * 2**20),
        cost_estimate=pl.CostEstimate(
            flops=4 * WINDOW * WINDOW * HALF,
            bytes_accessed=4 * WINDOW * WINDOW + 6 * WINDOW * HALF,
            transcendentals=0,
        ),
    )(high, low, x)


def mix_kernel(
    core, high, low, back, taps, spec, signal, gate, residual, skip, kept, sent, sums, prod
):
    filt = jnp.concatenate([taps[q] for q in range(Y)], axis=1)
    for tile in range(BINS // TILE):
        real = slice(tile * TILE, (tile + 1) * TILE)
        imag = slice(BINS + tile * TILE, BINS + (tile + 1) * TILE)
        fr = dot(high[real, :], filt) + dot(low[real, :], filt)
        fi = dot(high[imag, :], filt) + dot(low[imag, :], filt)
        sr = spec[real, :]
        si = spec[imag, :]
        cross = si * fi
        pr = sr * fr - cross
        pi = sr * fi + si * fr
        if tile == 0:
            first = lax.broadcasted_iota(jnp.int32, (TILE, HALF), 0) == 0
            pr = jnp.where(first, sr * fr, pr)
            pi = jnp.where(first, cross, pi)
        prod[real, :] = pr.astype(jnp.bfloat16)
        prod[imag, :] = pi.astype(jnp.bfloat16)
    for block in range(2):
        rows = slice(block * BLOCK, (block + 1) * BLOCK)
        conv = dot(back[rows, :], prod[...])
        x = signal[rows, :].astype(jnp.float32)
        weight = skip[...].astype(jnp.float32)
        mixed = gate[rows, :].astype(jnp.float32) * (conv + weight * x)
        updated = (residual[rows, :].astype(jnp.float32) + mixed).astype(jnp.bfloat16)
        wide = updated.astype(jnp.float32)
        total = jnp.sum(wide * wide, axis=1)
        for other in range(8):
            sums[2 * other + block, :] = total

        @pl.when(core[0] == block)
        def _():
            kept[...] = updated

        @pl.when(core[0] != block)
        def _():
            sent[...] = updated


def mix(core, high, low, back, taps, spec, signal, gate, residual, skip):
    vmem = pl.BlockSpec(memory_space=pltpu.VMEM)
    return pl.pallas_call(
        mix_kernel,
        out_shape=(
            jax.ShapeDtypeStruct((BLOCK, HALF), jnp.bfloat16),
            jax.ShapeDtypeStruct((BLOCK, HALF), jnp.bfloat16),
            jax.ShapeDtypeStruct((16, BLOCK), jnp.float32),
        ),
        in_specs=[pl.BlockSpec(memory_space=pltpu.SMEM)] + [vmem] * 9,
        out_specs=(vmem, vmem, vmem),
        scratch_shapes=[pltpu.VMEM((WINDOW, HALF), jnp.bfloat16)],
        compiler_params=pltpu.CompilerParams(vmem_limit_bytes=24 * 2**20),
        cost_estimate=pl.CostEstimate(
            flops=4 * WINDOW * LAGS * HALF + 2 * WINDOW * 2 * BLOCK * HALF,
            bytes_accessed=4 * WINDOW * LAGS + 4 * WINDOW * HALF,
            transcendentals=0,
        ),
    )(core, high, low, back, taps, spec, signal, gate, residual, skip)


def local(signal, gate, filter_taps, skip, residual, gain):
    (high, low), (back, _) = tables()
    index = lax.axis_index("ctx")
    y, z, core = index // (Z * CORES), index // CORES % Z, index % CORES
    lead = core == 0

    def mine(x):
        return lax.dynamic_slice_in_dim(x, core * HALF, HALF, axis=1)

    def others(x):
        return lax.dynamic_slice_in_dim(x, (1 - core) * HALF, HALF, axis=1)

    def ordered(own, other):
        return jnp.concatenate([jnp.where(lead, own, other), jnp.where(lead, other, own)], axis=0)

    def swap(x):
        return move(others(x), lambda y, z, c: (y, z, 1 - c))

    def halves(x):
        return ordered(mine(x), swap(x))

    taps_other = move(
        others(filter_taps), lambda y, z, c: (y, z, 1 - c) if y == 0 and z < 2 else None
    )
    current = halves(signal)
    held = ordered(mine(filter_taps), taps_other)
    piece = [held[:, q * QUARTER : (q + 1) * QUARTER] for q in range(Y)]
    parts = [
        move(piece[q], lambda y, z, c, q=q: (q, z, c) if y == 0 and z < 2 else None)
        for q in (2, 1, 3)
    ]
    earlier = move(current, lambda y, z, c: (y, z + 1, c) if z < Z - 1 else (y + 1, 0, c))
    held = jnp.where(y == 0, piece[0], parts[0] + parts[1] + parts[2])
    got = move(held, lambda y, z, c: (y, z + 4, c) if z < 2 else None)
    held = jnp.where(z < 4, held, got)
    got = move(held, lambda y, z, c: (y, z + 2, c) if z % 4 < 2 else None)
    held = jnp.where(z % 4 < 2, held, got)
    first = move(
        earlier[BLOCK:], lambda y, z, c: (y, z + 1, c) if z < Z - 1 else (y + 1, 0, c)
    )
    got = move(held, lambda y, z, c: (y, z ^ 1, c))
    even = z % 2 == 0
    quarter = jnp.concatenate(
        [jnp.where(even, held, got), jnp.where(even, got, held)[:BLOCK]], axis=0
    )
    gates = halves(gate)
    residuals = halves(residual)
    spec = spectrum(high, low, jnp.concatenate([first, earlier, current], axis=0))
    groups = [[(a * Z + b) * CORES + c for a in range(Y)] for b in range(Z) for c in range(CORES)]
    taps = lax.all_gather(quarter, "ctx", axis_index_groups=groups)
    skips = lax.dynamic_slice_in_dim(skip, core * HALF, HALF)[None, :]
    kept, sent, sums = mix(
        core.astype(jnp.int32)[None],
        high[:, :LAGS],
        low[:, :LAGS],
        back,
        taps,
        spec,
        current,
        gates,
        residuals,
        skips,
    )
    received = move(sent, lambda y, z, c: (y, z, 1 - c))
    size = Y * Z * CORES
    groups = [
        [a * size + b * CORES + c for a in range(8) for c in range(CORES)] for b in range(Y * Z)
    ]
    squares = jnp.sum(
        lax.all_to_all(sums, ("ch", "ctx"), 0, 0, axis_index_groups=groups), axis=0
    )
    new_residual = jnp.concatenate(
        [jnp.where(lead, kept, received), jnp.where(lead, received, kept)], axis=1
    )
    scale = lax.rsqrt(squares / D + EPS)[:, None]
    normed = new_residual.astype(jnp.float32) * scale * gain.astype(jnp.float32)[None, :]
    return (new_residual, normed.astype(jnp.bfloat16))


def solution(mesh):
    placed = (P("ctx", "ch"), P("ctx", "ch"), P("ctx", "ch"), P("ch"), P("ctx", "ch"), P("ch"))
    return jax.shard_map(
        local,
        mesh=mesh,
        in_specs=placed,
        out_specs=(P("ctx", "ch"), P("ctx", "ch")),
        check_vma=False,
    )
```

```python
import functools
import math

import jax
import jax.numpy as jnp
import ml_dtypes
import numpy as np
from jax import lax
from jax.experimental import pallas as pl
from jax.experimental.pallas import tpu as pltpu
from jax.sharding import PartitionSpec as P

D = 8192
BLOCK = 256
PANELS = 3
HALF = 512
QUARTER = 128
LAGS = PANELS * BLOCK
WINDOW = LAGS + 2 * BLOCK
BINS = WINDOW // 2
TILE = 128
EPS = 1e-05
Y, Z, CORES = 4, 8, 2


@functools.cache
def tables():
    bins = np.arange(BINS)[:, None]
    points = np.arange(WINDOW)[None, :]
    angle = (bins * points % WINDOW) * (2 * math.pi / WINDOW)
    real = np.cos(angle)
    imag = -np.sin(angle)
    imag[0] = (1.0 - 2.0 * (points % 2))[0]
    forward = np.concatenate([real, imag], axis=0)
    scale = np.where(np.arange(BINS) == 0, 1.0, 2.0)[:, None] / WINDOW
    back = np.concatenate([real * scale, imag * scale], axis=0).T[LAGS:]
    return tuple(x.astype(np.float32).astype(ml_dtypes.bfloat16) for x in (forward, back))


def pairs(rule):
    result = []
    for index in range(Y * Z * CORES):
        target = rule(index // (Z * CORES), index // CORES % Z, index % CORES)
        if target is not None:
            y, z, core = target
            result.append((index, y % Y * Z * CORES + z * CORES + core))
    return result


def move(x, rule):
    return lax.ppermute(x, "ctx", pairs(rule))


def dot(a, b):
    return jnp.dot(a, b, preferred_element_type=jnp.float32)


VMEM = pl.BlockSpec(memory_space=pltpu.VMEM)
SMEM = pl.BlockSpec(memory_space=pltpu.SMEM)
HBM = pl.BlockSpec(memory_space=pltpu.HBM)
LIMIT = pltpu.CompilerParams(vmem_limit_bytes=24 * 2**20)


def shaped(*shape, dtype=jnp.bfloat16):
    return jax.ShapeDtypeStruct(shape, dtype)


def columns(which):
    return pl.ds(pl.multiple_of(which * HALF, HALF), HALF)


def others_kernel(core, first, second, out, sems):
    there = columns(1 - core[0])
    copies = [
        pltpu.make_async_copy(x.at[:, there], out.at[i], sems.at[i])
        for i, x in enumerate((first, second))
    ]
    for copy in copies:
        copy.start()
    for copy in copies:
        copy.wait()


def others(core, first, second):
    return pl.pallas_call(
        others_kernel,
        out_shape=shaped(2, BLOCK, HALF),
        in_specs=[SMEM, HBM, HBM],
        out_specs=VMEM,
        scratch_shapes=[pltpu.SemaphoreType.DMA((2,))],
        compiler_params=LIMIT,
    )(core, first, second)


def prepare_kernel(core, taps, signal, other, both, even, odd, *pieces):
    own_rows = pl.ds(pl.multiple_of(core[0] * BLOCK, BLOCK), BLOCK)
    other_rows = pl.ds(pl.multiple_of((1 - core[0]) * BLOCK, BLOCK), BLOCK)
    for q, piece in enumerate(pieces):
        start = pl.multiple_of(core[0] * HALF + q * QUARTER, QUARTER)
        piece[own_rows, :] = taps[:, pl.ds(start, QUARTER)]
        piece[other_rows, :] = other[0, :, q * QUARTER : (q + 1) * QUARTER]

    @pl.when(core[0] == 0)
    def _():
        even[...] = signal[:, :HALF]
        odd[...] = other[1]

    @pl.when(core[0] == 1)
    def _():
        even[...] = other[1]
        odd[...] = signal[:, HALF:]

    both[0] = even[...]
    both[1] = odd[...]


def prepare(core, taps, signal, other):
    return pl.pallas_call(
        prepare_kernel,
        out_shape=(shaped(2, BLOCK, HALF),)
        + (shaped(BLOCK, HALF),) * 2
        + (shaped(2 * BLOCK, QUARTER),) * Y,
        in_specs=[SMEM, VMEM, VMEM, VMEM],
        out_specs=(VMEM,) * (3 + Y),
        compiler_params=LIMIT,
    )(core, taps, signal, other)


def join_kernel(place, held, got, extra, out):
    even = place[0] % 2 == 0

    @pl.when(even)
    def _():
        out[: 2 * BLOCK, :] = held[...]

    @pl.when(jnp.logical_not(even))
    def _():
        out[: 2 * BLOCK, :] = got[...]
        out[2 * BLOCK :, :] = held[:BLOCK, :]

    @pl.when(place[0] == 0)
    def _():
        out[2 * BLOCK :, :] = extra[...]

    @pl.when(jnp.logical_and(even, place[0] > 0))
    def _():
        out[2 * BLOCK :, :] = got[:BLOCK, :]


def join(place, held, got, extra):
    return pl.pallas_call(
        join_kernel,
        out_shape=shaped(LAGS, QUARTER),
        in_specs=[SMEM] + [VMEM] * 3,
        out_specs=VMEM,
        compiler_params=LIMIT,
        cost_estimate=pl.CostEstimate(
            flops=4 * WINDOW * WINDOW * HALF, bytes_accessed=0, transcendentals=0
        ),
    )(place, held, got, extra)


def mix_kernel(
    core,
    place,
    forward,
    back,
    taps,
    far,
    first,
    wrapped,
    before_even,
    before_odd,
    even,
    odd,
    gate,
    residual,
    other_both,
    skip,
    kept,
    sent,
    sums,
    window,
    prod,
):
    filt = jnp.concatenate([taps[q] for q in range(Y)], axis=1)
    window[:BLOCK, :] = jnp.where(place[0] < 2, far[...], first[...])
    window[BLOCK : 2 * BLOCK, :] = jnp.where(place[0] == 0, wrapped[0], before_even[...])
    window[2 * BLOCK : LAGS, :] = jnp.where(place[0] == 0, wrapped[1], before_odd[...])
    window[LAGS : LAGS + BLOCK, :] = even[...]
    window[LAGS + BLOCK :, :] = odd[...]
    for tile in range(BINS // TILE):
        real = slice(tile * TILE, (tile + 1) * TILE)
        imag = slice(BINS + tile * TILE, BINS + (tile + 1) * TILE)
        sr = dot(forward[real, :], window[...])
        si = dot(forward[imag, :], window[...])
        fr = dot(forward[real, :LAGS], filt)
        fi = dot(forward[imag, :LAGS], filt)
        cross = si * fi
        pr = sr * fr - cross
        pi = sr * fi + si * fr
        if tile == 0:
            lowest = lax.broadcasted_iota(jnp.int32, (TILE, HALF), 0) == 0
            pr = jnp.where(lowest, sr * fr, pr)
            pi = jnp.where(lowest, cross, pi)
        prod[real, :] = pr.astype(jnp.bfloat16)
        prod[imag, :] = pi.astype(jnp.bfloat16)
    here = columns(core[0])
    weight = skip[:, here].astype(jnp.float32)

    def update(block, x, g, r, out):
        rows = pl.ds(pl.multiple_of(block * BLOCK, BLOCK), BLOCK)
        conv = dot(back[rows, :], prod[...])
        mixed = g.astype(jnp.float32) * (conv + weight * x.astype(jnp.float32))
        updated = (r.astype(jnp.float32) + mixed).astype(jnp.bfloat16)
        wide = updated.astype(jnp.float32)
        out[...] = updated
        total = jnp.sum(wide * wide, axis=1)[None, :]
        for other in range(8):
            sums[2 * other + block] = total

    lead = core[0] == 0
    theirs = jnp.where(lead, odd[...], even[...])
    ours = jnp.where(lead, even[...], odd[...])
    update(1 - core[0], theirs, other_both[0], other_both[1], sent)
    update(core[0], ours, gate[:, here], residual[:, here], kept)


def mix(core, place, *arrays):
    return pl.pallas_call(
        mix_kernel,
        out_shape=(
            shaped(BLOCK, HALF),
            shaped(BLOCK, HALF),
            shaped(16, 1, BLOCK, dtype=jnp.float32),
        ),
        in_specs=[SMEM, SMEM] + [VMEM] * len(arrays),
        out_specs=(VMEM,) * 3,
        scratch_shapes=[pltpu.VMEM((WINDOW, HALF), jnp.bfloat16)] * 2,
        compiler_params=LIMIT,
        cost_estimate=pl.CostEstimate(
            flops=2 * WINDOW * (WINDOW + LAGS + 2 * BLOCK) * HALF,
            bytes_accessed=2 * WINDOW * LAGS + 4 * WINDOW * HALF,
            transcendentals=0,
        ),
    )(core, place, *arrays)


def finish_kernel(core, kept, received, sums, gain, updated, normed):
    total = sums[0]
    for other in range(1, 16):
        total = total + sums[other]
    scale = lax.rsqrt(total / D + EPS)
    scale = jnp.broadcast_to(scale, (8, BLOCK)).T[:, :1]
    for which, x in ((core[0], kept), (1 - core[0], received)):
        there = columns(which)
        values = x[...].astype(jnp.float32) * scale * gain[:, there].astype(jnp.float32)
        updated[:, there] = x[...]
        normed[:, there] = values.astype(jnp.bfloat16)


def finish(core, kept, received, sums, gain):
    return pl.pallas_call(
        finish_kernel,
        out_shape=(shaped(BLOCK, 2 * HALF),) * 2,
        in_specs=[SMEM] + [VMEM] * 4,
        out_specs=(VMEM, VMEM),
        compiler_params=LIMIT,
    )(core, kept, received, sums, gain)


def local(signal, gate, filter_taps, skip, residual, gain):
    forward, back = tables()
    index = lax.axis_index("ctx")
    y, z, core = index // (Z * CORES), index // CORES % Z, index % CORES
    lead = core == 0

    def flag(x):
        return x.astype(jnp.int32)[None]

    def swap(x):
        return move(x, lambda y, z, c: (y, z, 1 - c))

    other = swap(others(flag(core), filter_taps, signal))
    both, even, odd, *piece = prepare(flag(core), filter_taps, signal, other)
    parts = [
        move(piece[q], lambda y, z, c, q=q: (q, z, c) if y == 0 and z < 2 else None)
        for q in (1, 3, 2)
    ]

    before_odd = move(odd, lambda y, z, c: (y, z + 1, c) if z < Z - 1 else None)
    before_even = move(even, lambda y, z, c: (y, z + 1, c) if z < Z - 1 else None)
    wrapped = move(both, lambda y, z, c: (y + 1, 0, c) if z == Z - 1 else None)
    far = move(odd, lambda y, z, c: (y + 1, z - 6, c) if z >= Z - 2 else None)
    held = jnp.where(y == 0, piece[0], parts[0] + parts[1] + parts[2])
    extra = move(held[:BLOCK], lambda y, z, c: (y, 0, c) if z == 1 else None)
    got = move(held, lambda y, z, c: (y, z + 4, c) if z < 2 else None)
    held = jnp.where(z < 4, held, got)
    got = move(held, lambda y, z, c: (y, z + 2, c) if z % 4 < 2 else None)
    held = jnp.where(z % 4 < 2, held, got)
    first = move(before_odd, lambda y, z, c: (y, z + 1, c) if 0 < z < Z - 1 else None)
    other_both = swap(others(flag(core), gate, residual))
    got = move(held, lambda y, z, c: (y, z + 1, c) if z < Z - 1 else None)
    got, wrapped = lax.optimization_barrier((got, wrapped))
    quarter = join(flag(z), held, got, extra)
    groups = [[(a * Z + b) * CORES + c for a in range(Y)] for b in range(Z) for c in range(CORES)]
    taps = lax.all_gather(quarter, "ctx", axis_index_groups=groups)
    kept, sent, sums = mix(
        flag(core),
        flag(z),
        forward,
        back,
        taps,
        far,
        first,
        wrapped,
        before_even,
        before_odd,
        even,
        odd,
        gate,
        residual,
        other_both,
        skip[None, :],
    )
    size = Y * Z * CORES
    groups = [
        [a * size + b * CORES + c for a in range(8) for c in range(CORES)] for b in range(Y * Z)
    ]
    squares = lax.all_to_all(sums, ("ch", "ctx"), 0, 0, axis_index_groups=groups)
    return finish(flag(core), kept, swap(sent), squares, gain[None, :])


def solution(mesh):
    placed = (P("ctx", "ch"), P("ctx", "ch"), P("ctx", "ch"), P("ch"), P("ctx", "ch"), P("ch"))
    return jax.shard_map(
        local,
        mesh=mesh,
        in_specs=placed,
        out_specs=(P("ctx", "ch"), P("ctx", "ch")),
        check_vma=False,
    )
```

```python
import functools
import math

import jax
import jax.numpy as jnp
import ml_dtypes
import numpy as np
from jax import lax
from jax.experimental import pallas as pl
from jax.experimental.pallas import tpu as pltpu
from jax.sharding import PartitionSpec as P

D = 8192
BLOCK = 256
PANELS = 3
HALF = 512
QUARTER = 128
LAGS = PANELS * BLOCK
WINDOW = LAGS + 2 * BLOCK
BINS = WINDOW // 2
TILE = 128
EPS = 1e-05
Y, Z, CORES = 4, 8, 2


@functools.cache
def tables():
    bins = np.arange(BINS)[:, None]
    points = np.arange(WINDOW)[None, :]
    angle = (bins * points % WINDOW) * (2 * math.pi / WINDOW)
    real = np.cos(angle)
    imag = -np.sin(angle)
    imag[0] = (1.0 - 2.0 * (points % 2))[0]
    forward = np.concatenate([real, imag], axis=0)
    scale = np.where(np.arange(BINS) == 0, 1.0, 2.0)[:, None] / WINDOW
    back = np.concatenate([real * scale, imag * scale], axis=0).T[LAGS:]
    return tuple(x.astype(np.float32).astype(ml_dtypes.bfloat16) for x in (forward, back))


def pairs(rule):
    result = []
    for index in range(Y * Z * CORES):
        target = rule(index // (Z * CORES), index // CORES % Z, index % CORES)
        if target is not None:
            y, z, core = target
            result.append((index, y % Y * Z * CORES + z * CORES + core))
    return result


def move(x, rule):
    return lax.ppermute(x, "ctx", pairs(rule))


def dot(a, b):
    return jnp.dot(a, b, preferred_element_type=jnp.float32)


VMEM = pl.BlockSpec(memory_space=pltpu.VMEM)
SMEM = pl.BlockSpec(memory_space=pltpu.SMEM)
HBM = pl.BlockSpec(memory_space=pltpu.HBM)
LIMIT = pltpu.CompilerParams(vmem_limit_bytes=24 * 2**20)


def shaped(*shape, dtype=jnp.bfloat16):
    return jax.ShapeDtypeStruct(shape, dtype)


def columns(which):
    return pl.ds(pl.multiple_of(which * HALF, HALF), HALF)


def others_kernel(core, first, second, out, sems):
    there = columns(1 - core[0])
    copies = [
        pltpu.make_async_copy(x.at[:, there], out.at[i], sems.at[i])
        for i, x in enumerate((first, second))
    ]
    for copy in copies:
        copy.start()
    for copy in copies:
        copy.wait()


def others(core, first, second):
    return pl.pallas_call(
        others_kernel,
        out_shape=shaped(2, BLOCK, HALF),
        in_specs=[SMEM, HBM, HBM],
        out_specs=VMEM,
        scratch_shapes=[pltpu.SemaphoreType.DMA((2,))],
        compiler_params=LIMIT,
    )(core, first, second)


def prepare_kernel(core, taps, signal, other, both, even, odd, *pieces):
    own_rows = pl.ds(pl.multiple_of(core[0] * BLOCK, BLOCK), BLOCK)
    other_rows = pl.ds(pl.multiple_of((1 - core[0]) * BLOCK, BLOCK), BLOCK)
    for q, piece in enumerate(pieces):
        start = pl.multiple_of(core[0] * HALF + q * QUARTER, QUARTER)
        piece[own_rows, :] = taps[:, pl.ds(start, QUARTER)]
        piece[other_rows, :] = other[0, :, q * QUARTER : (q + 1) * QUARTER]

    @pl.when(core[0] == 0)
    def _():
        even[...] = signal[:, :HALF]
        odd[...] = other[1]

    @pl.when(core[0] == 1)
    def _():
        even[...] = other[1]
        odd[...] = signal[:, HALF:]

    both[0] = even[...]
    both[1] = odd[...]


def prepare(core, taps, signal, other):
    return pl.pallas_call(
        prepare_kernel,
        out_shape=(shaped(2, BLOCK, HALF),)
        + (shaped(BLOCK, HALF),) * 2
        + (shaped(2 * BLOCK, QUARTER),) * Y,
        in_specs=[SMEM, VMEM, VMEM, VMEM],
        out_specs=(VMEM,) * (3 + Y),
        compiler_params=LIMIT,
    )(core, taps, signal, other)


def join_kernel(place, held, got, extra, out):
    even = place[0] % 2 == 0

    @pl.when(even)
    def _():
        out[: 2 * BLOCK, :] = held[...]

    @pl.when(jnp.logical_not(even))
    def _():
        out[: 2 * BLOCK, :] = got[...]
        out[2 * BLOCK :, :] = held[:BLOCK, :]

    @pl.when(place[0] == 0)
    def _():
        out[2 * BLOCK :, :] = extra[...]

    @pl.when(jnp.logical_and(even, place[0] > 0))
    def _():
        out[2 * BLOCK :, :] = got[:BLOCK, :]


def join(place, held, got, extra):
    return pl.pallas_call(
        join_kernel,
        out_shape=shaped(LAGS, QUARTER),
        in_specs=[SMEM] + [VMEM] * 3,
        out_specs=VMEM,
        compiler_params=LIMIT,
        cost_estimate=pl.CostEstimate(
            flops=4 * WINDOW * WINDOW * HALF, bytes_accessed=0, transcendentals=0
        ),
    )(place, held, got, extra)


def mix_kernel(
    core,
    place,
    forward,
    back,
    taps,
    far,
    first,
    wrapped,
    before_even,
    before_odd,
    even,
    odd,
    gate,
    residual,
    other_both,
    skip,
    kept,
    sent,
    sums,
    window,
    prod,
):
    filt = jnp.concatenate([taps[q] for q in range(Y)], axis=1)
    window[:BLOCK, :] = jnp.where(place[0] < 2, far[...], first[...])
    window[BLOCK : 2 * BLOCK, :] = jnp.where(place[0] == 0, wrapped[0], before_even[...])
    window[2 * BLOCK : LAGS, :] = jnp.where(place[0] == 0, wrapped[1], before_odd[...])
    window[LAGS : LAGS + BLOCK, :] = even[...]
    window[LAGS + BLOCK :, :] = odd[...]
    for tile in range(BINS // TILE):
        real = slice(tile * TILE, (tile + 1) * TILE)
        imag = slice(BINS + tile * TILE, BINS + (tile + 1) * TILE)
        sr = dot(forward[real, :], window[...])
        si = dot(forward[imag, :], window[...])
        fr = dot(forward[real, :LAGS], filt)
        fi = dot(forward[imag, :LAGS], filt)
        cross = si * fi
        pr = sr * fr - cross
        pi = sr * fi + si * fr
        if tile == 0:
            lowest = lax.broadcasted_iota(jnp.int32, (TILE, HALF), 0) == 0
            pr = jnp.where(lowest, sr * fr, pr)
            pi = jnp.where(lowest, cross, pi)
        prod[real, :] = pr.astype(jnp.bfloat16)
        prod[imag, :] = pi.astype(jnp.bfloat16)
    here = columns(core[0])
    weight = skip[:, here].astype(jnp.float32)

    def update(block, x, g, r, out):
        rows = pl.ds(pl.multiple_of(block * BLOCK, BLOCK), BLOCK)
        conv = dot(back[rows, :], prod[...])
        mixed = g.astype(jnp.float32) * (conv + weight * x.astype(jnp.float32))
        updated = (r.astype(jnp.float32) + mixed).astype(jnp.bfloat16)
        wide = updated.astype(jnp.float32)
        out[...] = updated
        total = jnp.sum(wide * wide, axis=1)[None, :]
        for other in range(8):
            sums[2 * other + block] = total

    lead = core[0] == 0
    theirs = jnp.where(lead, odd[...], even[...])
    ours = jnp.where(lead, even[...], odd[...])
    update(1 - core[0], theirs, other_both[0], other_both[1], sent)
    update(core[0], ours, gate[:, here], residual[:, here], kept)


def mix(core, place, *arrays):
    return pl.pallas_call(
        mix_kernel,
        out_shape=(
            shaped(BLOCK, HALF),
            shaped(BLOCK, HALF),
            shaped(16, 1, BLOCK, dtype=jnp.float32),
        ),
        in_specs=[SMEM, SMEM] + [VMEM] * len(arrays),
        out_specs=(VMEM,) * 3,
        scratch_shapes=[pltpu.VMEM((WINDOW, HALF), jnp.bfloat16)] * 2,
        compiler_params=LIMIT,
        cost_estimate=pl.CostEstimate(
            flops=2 * WINDOW * (WINDOW + LAGS + 2 * BLOCK) * HALF,
            bytes_accessed=2 * WINDOW * LAGS + 4 * WINDOW * HALF,
            transcendentals=0,
        ),
    )(core, place, *arrays)


def finish_kernel(core, kept, received, sums, gain, updated, normed):
    total = sums[0]
    for other in range(1, 16):
        total = total + sums[other]
    scale = lax.rsqrt(total / D + EPS)
    scale = jnp.broadcast_to(scale, (8, BLOCK)).T[:, :1]
    for which, x in ((core[0], kept), (1 - core[0], received)):
        there = columns(which)
        values = x[...].astype(jnp.float32) * scale * gain[:, there].astype(jnp.float32)
        updated[:, there] = x[...]
        normed[:, there] = values.astype(jnp.bfloat16)


def finish(core, kept, received, sums, gain):
    return pl.pallas_call(
        finish_kernel,
        out_shape=(shaped(BLOCK, 2 * HALF),) * 2,
        in_specs=[SMEM] + [VMEM] * 4,
        out_specs=(VMEM, VMEM),
        compiler_params=LIMIT,
    )(core, kept, received, sums, gain)


def local(signal, gate, filter_taps, skip, residual, gain):
    forward, back = tables()
    index = lax.axis_index("ctx")
    y, z, core = index // (Z * CORES), index // CORES % Z, index % CORES
    lead = core == 0

    def flag(x):
        return x.astype(jnp.int32)[None]

    def swap(x):
        return move(x, lambda y, z, c: (y, z, 1 - c))

    other = swap(others(flag(core), filter_taps, signal))
    both, even, odd, *piece = prepare(flag(core), filter_taps, signal, other)
    parts = [
        move(piece[q], lambda y, z, c, q=q: (q, z, c) if y == 0 and z < 2 else None)
        for q in (1, 3, 2)
    ]

    before_odd = move(odd, lambda y, z, c: (y, z + 1, c) if z < Z - 1 else None)
    before_even = move(even, lambda y, z, c: (y, z + 1, c) if z < Z - 1 else None)
    wrapped = move(both, lambda y, z, c: (y + 1, 0, c) if z == Z - 1 else None)
    far = move(odd, lambda y, z, c: (y + 1, z - 6, c) if z >= Z - 2 else None)
    held = jnp.where(y == 0, piece[0], parts[0] + parts[1] + parts[2])
    extra = move(held[:BLOCK], lambda y, z, c: (y, 0, c) if z == 1 else None)
    got = move(held, lambda y, z, c: (y, z + 4, c) if z < 2 else None)
    held = jnp.where(z < 4, held, got)
    held, extra = lax.optimization_barrier((held, extra))
    got = move(held, lambda y, z, c: (y, z + 2, c) if z % 4 < 2 else None)
    held = jnp.where(z % 4 < 2, held, got)
    first = move(before_odd, lambda y, z, c: (y, z + 1, c) if 0 < z < Z - 1 else None)
    other_both = swap(others(flag(core), gate, residual))
    got = move(held, lambda y, z, c: (y, z + 1, c) if z < Z - 1 else None)
    got, wrapped = lax.optimization_barrier((got, wrapped))
    quarter = join(flag(z), held, got, extra)
    groups = [[(a * Z + b) * CORES + c for a in range(Y)] for b in range(Z) for c in range(CORES)]
    taps = lax.all_gather(quarter, "ctx", axis_index_groups=groups)
    kept, sent, sums = mix(
        flag(core),
        flag(z),
        forward,
        back,
        taps,
        far,
        first,
        wrapped,
        before_even,
        before_odd,
        even,
        odd,
        gate,
        residual,
        other_both,
        skip[None, :],
    )
    size = Y * Z * CORES
    groups = [
        [a * size + b * CORES + c for a in range(8) for c in range(CORES)] for b in range(Y * Z)
    ]
    squares = lax.all_to_all(sums, ("ch", "ctx"), 0, 0, axis_index_groups=groups)
    return finish(flag(core), kept, swap(sent), squares, gain[None, :])


def solution(mesh):
    placed = (P("ctx", "ch"), P("ctx", "ch"), P("ctx", "ch"), P("ch"), P("ctx", "ch"), P("ch"))
    return jax.shard_map(
        local,
        mesh=mesh,
        in_specs=placed,
        out_specs=(P("ctx", "ch"), P("ctx", "ch")),
        check_vma=False,
    )
```

```python
import functools
import math

import jax
import jax.numpy as jnp
import ml_dtypes
import numpy as np
from jax import lax
from jax.experimental import pallas as pl
from jax.experimental.pallas import tpu as pltpu
from jax.sharding import PartitionSpec as P

D = 8192
BLOCK = 256
PANELS = 3
HALF = 512
QUARTER = 128
LAGS = PANELS * BLOCK
WINDOW = LAGS + 2 * BLOCK
BINS = WINDOW // 2
TILE = 128
EPS = 1e-05
Y, Z, CORES = 4, 8, 2


@functools.cache
def tables():
    bins = np.arange(BINS)[:, None]
    points = np.arange(WINDOW)[None, :]
    angle = (bins * points % WINDOW) * (2 * math.pi / WINDOW)
    real = np.cos(angle)
    imag = -np.sin(angle)
    imag[0] = (1.0 - 2.0 * (points % 2))[0]
    forward = np.concatenate([real, imag], axis=0)
    scale = np.where(np.arange(BINS) == 0, 1.0, 2.0)[:, None] / WINDOW
    back = np.concatenate([real * scale, imag * scale], axis=0).T[LAGS:]
    return tuple(x.astype(np.float32).astype(ml_dtypes.bfloat16) for x in (forward, back))


def pairs(rule):
    result = []
    for index in range(Y * Z * CORES):
        target = rule(index // (Z * CORES), index // CORES % Z, index % CORES)
        if target is not None:
            y, z, core = target
            result.append((index, y % Y * Z * CORES + z * CORES + core))
    return result


def move(x, rule):
    return lax.ppermute(x, "ctx", pairs(rule))


def dot(a, b):
    return jnp.dot(a, b, preferred_element_type=jnp.float32)


VMEM = pl.BlockSpec(memory_space=pltpu.VMEM)
SMEM = pl.BlockSpec(memory_space=pltpu.SMEM)
HBM = pl.BlockSpec(memory_space=pltpu.HBM)
LIMIT = pltpu.CompilerParams(vmem_limit_bytes=24 * 2**20)


def shaped(*shape, dtype=jnp.bfloat16):
    return jax.ShapeDtypeStruct(shape, dtype)


def columns(which):
    return pl.ds(pl.multiple_of(which * HALF, HALF), HALF)


def others_kernel(core, first, second, out, sems):
    there = columns(1 - core[0])
    copies = [
        pltpu.make_async_copy(x.at[:, there], out.at[i], sems.at[i])
        for i, x in enumerate((first, second))
    ]
    for copy in copies:
        copy.start()
    for copy in copies:
        copy.wait()


def others(core, first, second):
    return pl.pallas_call(
        others_kernel,
        out_shape=shaped(2, BLOCK, HALF),
        in_specs=[SMEM, HBM, HBM],
        out_specs=VMEM,
        scratch_shapes=[pltpu.SemaphoreType.DMA((2,))],
        compiler_params=LIMIT,
    )(core, first, second)


def prepare_kernel(core, taps, signal, other, both, even, odd, *pieces):
    own_rows = pl.ds(pl.multiple_of(core[0] * BLOCK, BLOCK), BLOCK)
    other_rows = pl.ds(pl.multiple_of((1 - core[0]) * BLOCK, BLOCK), BLOCK)
    for q, piece in enumerate(pieces):
        start = pl.multiple_of(core[0] * HALF + q * QUARTER, QUARTER)
        piece[own_rows, :] = taps[:, pl.ds(start, QUARTER)]
        piece[other_rows, :] = other[0, :, q * QUARTER : (q + 1) * QUARTER]

    @pl.when(core[0] == 0)
    def _():
        even[...] = signal[:, :HALF]
        odd[...] = other[1]

    @pl.when(core[0] == 1)
    def _():
        even[...] = other[1]
        odd[...] = signal[:, HALF:]

    both[0] = even[...]
    both[1] = odd[...]


def prepare(core, taps, signal, other):
    return pl.pallas_call(
        prepare_kernel,
        out_shape=(shaped(2, BLOCK, HALF),)
        + (shaped(BLOCK, HALF),) * 2
        + (shaped(2 * BLOCK, QUARTER),) * Y,
        in_specs=[SMEM, VMEM, VMEM, VMEM],
        out_specs=(VMEM,) * (3 + Y),
        compiler_params=LIMIT,
    )(core, taps, signal, other)


def join_kernel(place, held, got, extra, out):
    even = place[0] % 2 == 0

    @pl.when(even)
    def _():
        out[: 2 * BLOCK, :] = held[...]

    @pl.when(jnp.logical_not(even))
    def _():
        out[: 2 * BLOCK, :] = got[...]
        out[2 * BLOCK :, :] = held[:BLOCK, :]

    @pl.when(place[0] == 0)
    def _():
        out[2 * BLOCK :, :] = extra[...]

    @pl.when(jnp.logical_and(even, place[0] > 0))
    def _():
        out[2 * BLOCK :, :] = got[:BLOCK, :]


def join(place, held, got, extra):
    return pl.pallas_call(
        join_kernel,
        out_shape=shaped(LAGS, QUARTER),
        in_specs=[SMEM] + [VMEM] * 3,
        out_specs=VMEM,
        compiler_params=LIMIT,
        cost_estimate=pl.CostEstimate(
            flops=4 * WINDOW * WINDOW * HALF, bytes_accessed=0, transcendentals=0
        ),
    )(place, held, got, extra)


def mix_kernel(
    core,
    place,
    forward,
    back,
    taps,
    far,
    first,
    wrapped,
    before_even,
    before_odd,
    even,
    odd,
    gate,
    residual,
    other_both,
    skip,
    kept,
    sent,
    sums,
    window,
    prod,
):
    filt = jnp.concatenate([taps[q] for q in range(Y)], axis=1)
    window[:BLOCK, :] = jnp.where(place[0] < 2, far[...], first[...])
    window[BLOCK : 2 * BLOCK, :] = jnp.where(place[0] == 0, wrapped[0], before_even[...])
    window[2 * BLOCK : LAGS, :] = jnp.where(place[0] == 0, wrapped[1], before_odd[...])
    window[LAGS : LAGS + BLOCK, :] = even[...]
    window[LAGS + BLOCK :, :] = odd[...]
    for tile in range(BINS // TILE):
        real = slice(tile * TILE, (tile + 1) * TILE)
        imag = slice(BINS + tile * TILE, BINS + (tile + 1) * TILE)
        sr = dot(forward[real, :], window[...])
        si = dot(forward[imag, :], window[...])
        fr = dot(forward[real, :LAGS], filt)
        fi = dot(forward[imag, :LAGS], filt)
        cross = si * fi
        pr = sr * fr - cross
        pi = sr * fi + si * fr
        if tile == 0:
            lowest = lax.broadcasted_iota(jnp.int32, (TILE, HALF), 0) == 0
            pr = jnp.where(lowest, sr * fr, pr)
            pi = jnp.where(lowest, cross, pi)
        prod[real, :] = pr.astype(jnp.bfloat16)
        prod[imag, :] = pi.astype(jnp.bfloat16)
    here = columns(core[0])
    weight = skip[:, here].astype(jnp.float32)

    def update(block, x, g, r, out):
        rows = pl.ds(pl.multiple_of(block * BLOCK, BLOCK), BLOCK)
        conv = dot(back[rows, :], prod[...])
        mixed = g.astype(jnp.float32) * (conv + weight * x.astype(jnp.float32))
        updated = (r.astype(jnp.float32) + mixed).astype(jnp.bfloat16)
        wide = updated.astype(jnp.float32)
        out[...] = updated
        total = jnp.sum(wide * wide, axis=1)[None, :]
        for other in range(8):
            sums[2 * other + block] = total

    lead = core[0] == 0
    theirs = jnp.where(lead, odd[...], even[...])
    ours = jnp.where(lead, even[...], odd[...])
    update(1 - core[0], theirs, other_both[0], other_both[1], sent)
    update(core[0], ours, gate[:, here], residual[:, here], kept)


def mix(core, place, *arrays):
    return pl.pallas_call(
        mix_kernel,
        out_shape=(
            shaped(BLOCK, HALF),
            shaped(BLOCK, HALF),
            shaped(16, 1, BLOCK, dtype=jnp.float32),
        ),
        in_specs=[SMEM, SMEM] + [VMEM] * len(arrays),
        out_specs=(VMEM,) * 3,
        scratch_shapes=[pltpu.VMEM((WINDOW, HALF), jnp.bfloat16)] * 2,
        compiler_params=LIMIT,
        cost_estimate=pl.CostEstimate(
            flops=2 * WINDOW * (WINDOW + LAGS + 2 * BLOCK) * HALF,
            bytes_accessed=2 * WINDOW * LAGS + 4 * WINDOW * HALF,
            transcendentals=0,
        ),
    )(core, place, *arrays)


def local(signal, gate, filter_taps, skip, residual, gain):
    forward, back = tables()
    index = lax.axis_index("ctx")
    y, z, core = index // (Z * CORES), index // CORES % Z, index % CORES
    lead = core == 0

    def flag(x):
        return x.astype(jnp.int32)[None]

    def swap(x):
        return move(x, lambda y, z, c: (y, z, 1 - c))

    other = swap(others(flag(core), filter_taps, signal))
    both, even, odd, *piece = prepare(flag(core), filter_taps, signal, other)
    parts = [
        move(piece[q], lambda y, z, c, q=q: (q, z, c) if y == 0 and z < 2 else None)
        for q in (1, 3, 2)
    ]

    before_odd = move(odd, lambda y, z, c: (y, z + 1, c) if z < Z - 1 else None)
    before_even = move(even, lambda y, z, c: (y, z + 1, c) if z < Z - 1 else None)
    wrapped = move(both, lambda y, z, c: (y + 1, 0, c) if z == Z - 1 else None)
    far = move(odd, lambda y, z, c: (y + 1, z - 6, c) if z >= Z - 2 else None)
    held = jnp.where(y == 0, piece[0], parts[0] + parts[1] + parts[2])
    extra = move(held[:BLOCK], lambda y, z, c: (y, 0, c) if z == 1 else None)
    got = move(held, lambda y, z, c: (y, z + 4, c) if z < 2 else None)
    held = jnp.where(z < 4, held, got)
    held, extra = lax.optimization_barrier((held, extra))
    got = move(held, lambda y, z, c: (y, z + 2, c) if z % 4 < 2 else None)
    held = jnp.where(z % 4 < 2, held, got)
    first = move(before_odd, lambda y, z, c: (y, z + 1, c) if 0 < z < Z - 1 else None)
    other_both = swap(others(flag(core), gate, residual))
    got = move(held, lambda y, z, c: (y, z + 1, c) if z < Z - 1 else None)
    got, wrapped = lax.optimization_barrier((got, wrapped))
    quarter = join(flag(z), held, got, extra)
    groups = [[(a * Z + b) * CORES + c for a in range(Y)] for b in range(Z) for c in range(CORES)]
    taps = lax.all_gather(quarter, "ctx", axis_index_groups=groups)
    kept, sent, sums = mix(
        flag(core),
        flag(z),
        forward,
        back,
        taps,
        far,
        first,
        wrapped,
        before_even,
        before_odd,
        even,
        odd,
        gate,
        residual,
        other_both,
        skip[None, :],
    )
    size = Y * Z * CORES
    groups = [
        [a * size + b * CORES + c for a in range(8) for c in range(CORES)] for b in range(Y * Z)
    ]
    squares = lax.all_to_all(sums, ("ch", "ctx"), 0, 0, axis_index_groups=groups)
    received = swap(sent)
    lead = core == 0
    new_residual = jnp.concatenate(
        [jnp.where(lead, kept, received), jnp.where(lead, received, kept)], axis=1
    )
    scale = lax.rsqrt(jnp.sum(squares[:, 0], axis=0) / D + EPS)[:, None]
    normed = new_residual.astype(jnp.float32) * scale * gain.astype(jnp.float32)[None, :]
    return (new_residual, normed.astype(jnp.bfloat16))


def solution(mesh):
    placed = (P("ctx", "ch"), P("ctx", "ch"), P("ctx", "ch"), P("ch"), P("ctx", "ch"), P("ch"))
    return jax.shard_map(
        local,
        mesh=mesh,
        in_specs=placed,
        out_specs=(P("ctx", "ch"), P("ctx", "ch")),
        check_vma=False,
    )
```

```python
import functools
import math

import jax
import jax.numpy as jnp
import ml_dtypes
import numpy as np
from jax import lax
from jax.experimental import pallas as pl
from jax.experimental.pallas import tpu as pltpu
from jax.sharding import PartitionSpec as P

D = 8192
BLOCK = 256
PANELS = 3
HALF = 512
QUARTER = 128
LAGS = PANELS * BLOCK
WINDOW = LAGS + 2 * BLOCK
BINS = WINDOW // 2
TILE = 128
EPS = 1e-05
Y, Z, CORES = 4, 8, 2


@functools.cache
def tables():
    bins = np.arange(BINS)[:, None]
    points = np.arange(WINDOW)[None, :]
    angle = (bins * points % WINDOW) * (2 * math.pi / WINDOW)
    real = np.cos(angle)
    imag = -np.sin(angle)
    imag[0] = (1.0 - 2.0 * (points % 2))[0]
    forward = np.concatenate([real, imag], axis=0)
    scale = np.where(np.arange(BINS) == 0, 1.0, 2.0)[:, None] / WINDOW
    back = np.concatenate([real * scale, imag * scale], axis=0).T[LAGS:]
    return tuple(x.astype(np.float32).astype(ml_dtypes.bfloat16) for x in (forward, back))


def pairs(rule):
    result = []
    for index in range(Y * Z * CORES):
        target = rule(index // (Z * CORES), index // CORES % Z, index % CORES)
        if target is not None:
            y, z, core = target
            result.append((index, y % Y * Z * CORES + z * CORES + core))
    return result


def move(x, rule):
    return lax.ppermute(x, "ctx", pairs(rule))


def dot(a, b):
    return jnp.dot(a, b, preferred_element_type=jnp.float32)


VMEM = pl.BlockSpec(memory_space=pltpu.VMEM)
SMEM = pl.BlockSpec(memory_space=pltpu.SMEM)
HBM = pl.BlockSpec(memory_space=pltpu.HBM)
LIMIT = pltpu.CompilerParams(vmem_limit_bytes=24 * 2**20)


def shaped(*shape, dtype=jnp.bfloat16):
    return jax.ShapeDtypeStruct(shape, dtype)


def columns(which):
    return pl.ds(pl.multiple_of(which * HALF, HALF), HALF)


def others_kernel(core, first, second, out, sems):
    there = columns(1 - core[0])
    copies = [
        pltpu.make_async_copy(x.at[:, there], out.at[i], sems.at[i])
        for i, x in enumerate((first, second))
    ]
    for copy in copies:
        copy.start()
    for copy in copies:
        copy.wait()


def others(core, first, second):
    return pl.pallas_call(
        others_kernel,
        out_shape=shaped(2, BLOCK, HALF),
        in_specs=[SMEM, HBM, HBM],
        out_specs=VMEM,
        scratch_shapes=[pltpu.SemaphoreType.DMA((2,))],
        compiler_params=LIMIT,
    )(core, first, second)


def prepare_kernel(core, taps, signal, other, both, even, odd, *pieces):
    own_rows = pl.ds(pl.multiple_of(core[0] * BLOCK, BLOCK), BLOCK)
    other_rows = pl.ds(pl.multiple_of((1 - core[0]) * BLOCK, BLOCK), BLOCK)
    for q, piece in enumerate(pieces):
        start = pl.multiple_of(core[0] * HALF + q * QUARTER, QUARTER)
        piece[own_rows, :] = taps[:, pl.ds(start, QUARTER)]
        piece[other_rows, :] = other[0, :, q * QUARTER : (q + 1) * QUARTER]

    @pl.when(core[0] == 0)
    def _():
        even[...] = signal[:, :HALF]
        odd[...] = other[1]

    @pl.when(core[0] == 1)
    def _():
        even[...] = other[1]
        odd[...] = signal[:, HALF:]

    both[0] = even[...]
    both[1] = odd[...]


def prepare(core, taps, signal, other):
    return pl.pallas_call(
        prepare_kernel,
        out_shape=(shaped(2, BLOCK, HALF),)
        + (shaped(BLOCK, HALF),) * 2
        + (shaped(2 * BLOCK, QUARTER),) * Y,
        in_specs=[SMEM, VMEM, VMEM, VMEM],
        out_specs=(VMEM,) * (3 + Y),
        compiler_params=LIMIT,
    )(core, taps, signal, other)


def join_kernel(place, held, got, extra, out):
    even = place[0] % 2 == 0

    @pl.when(even)
    def _():
        out[: 2 * BLOCK, :] = held[...]

    @pl.when(jnp.logical_not(even))
    def _():
        out[: 2 * BLOCK, :] = got[...]
        out[2 * BLOCK :, :] = held[:BLOCK, :]

    @pl.when(place[0] == 0)
    def _():
        out[2 * BLOCK :, :] = extra[...]

    @pl.when(jnp.logical_and(even, place[0] > 0))
    def _():
        out[2 * BLOCK :, :] = got[:BLOCK, :]


def join(place, held, got, extra):
    return pl.pallas_call(
        join_kernel,
        out_shape=shaped(LAGS, QUARTER),
        in_specs=[SMEM] + [VMEM] * 3,
        out_specs=VMEM,
        compiler_params=LIMIT,
        cost_estimate=pl.CostEstimate(
            flops=4 * WINDOW * WINDOW * HALF, bytes_accessed=0, transcendentals=0
        ),
    )(place, held, got, extra)


def mix_kernel(
    core,
    place,
    forward,
    back,
    taps,
    far,
    first,
    wrapped,
    before_even,
    before_odd,
    even,
    odd,
    gate,
    residual,
    other_both,
    skip,
    kept,
    sent,
    sums,
    window,
    prod,
):
    filt = jnp.concatenate([taps[q] for q in range(Y)], axis=1)
    window[:BLOCK, :] = jnp.where(place[0] < 2, far[...], first[...])
    window[BLOCK : 2 * BLOCK, :] = jnp.where(place[0] == 0, wrapped[0], before_even[...])
    window[2 * BLOCK : LAGS, :] = jnp.where(place[0] == 0, wrapped[1], before_odd[...])
    window[LAGS : LAGS + BLOCK, :] = even[...]
    window[LAGS + BLOCK :, :] = odd[...]
    for tile in range(BINS // TILE):
        real = slice(tile * TILE, (tile + 1) * TILE)
        imag = slice(BINS + tile * TILE, BINS + (tile + 1) * TILE)
        sr = dot(forward[real, :], window[...])
        si = dot(forward[imag, :], window[...])
        fr = dot(forward[real, :LAGS], filt)
        fi = dot(forward[imag, :LAGS], filt)
        cross = si * fi
        pr = sr * fr - cross
        pi = sr * fi + si * fr
        if tile == 0:
            lowest = lax.broadcasted_iota(jnp.int32, (TILE, HALF), 0) == 0
            pr = jnp.where(lowest, sr * fr, pr)
            pi = jnp.where(lowest, cross, pi)
        prod[real, :] = pr.astype(jnp.bfloat16)
        prod[imag, :] = pi.astype(jnp.bfloat16)
    here = columns(core[0])
    weight = skip[:, here].astype(jnp.float32)

    def update(block, x, g, r, out):
        rows = pl.ds(pl.multiple_of(block * BLOCK, BLOCK), BLOCK)
        conv = dot(back[rows, :], prod[...])
        mixed = g.astype(jnp.float32) * (conv + weight * x.astype(jnp.float32))
        updated = (r.astype(jnp.float32) + mixed).astype(jnp.bfloat16)
        wide = updated.astype(jnp.float32)
        out[...] = updated
        total = jnp.sum(wide * wide, axis=1)[None, :]
        for other in range(8):
            sums[2 * other + block] = total

    lead = core[0] == 0
    theirs = jnp.where(lead, odd[...], even[...])
    ours = jnp.where(lead, even[...], odd[...])
    update(1 - core[0], theirs, other_both[0], other_both[1], sent)
    update(core[0], ours, gate[:, here], residual[:, here], kept)


def mix(core, place, *arrays):
    return pl.pallas_call(
        mix_kernel,
        out_shape=(
            shaped(BLOCK, HALF),
            shaped(BLOCK, HALF),
            shaped(16, 1, BLOCK, dtype=jnp.float32),
        ),
        in_specs=[SMEM, SMEM] + [VMEM] * len(arrays),
        out_specs=(VMEM,) * 3,
        scratch_shapes=[pltpu.VMEM((WINDOW, HALF), jnp.bfloat16)] * 2,
        compiler_params=LIMIT,
        cost_estimate=pl.CostEstimate(
            flops=2 * WINDOW * (WINDOW + LAGS + 2 * BLOCK) * HALF,
            bytes_accessed=2 * WINDOW * LAGS + 4 * WINDOW * HALF,
            transcendentals=0,
        ),
    )(core, place, *arrays)


def local(signal, gate, filter_taps, skip, residual, gain):
    forward, back = tables()
    index = lax.axis_index("ctx")
    y, z, core = index // (Z * CORES), index // CORES % Z, index % CORES
    lead = core == 0

    def flag(x):
        return x.astype(jnp.int32)[None]

    def swap(x):
        return move(x, lambda y, z, c: (y, z, 1 - c))

    other = swap(others(flag(core), filter_taps, signal))
    both, even, odd, *piece = prepare(flag(core), filter_taps, signal, other)
    parts = [
        move(piece[q], lambda y, z, c, q=q: (q, z, c) if y == 0 and z < 2 else None)
        for q in (1, 2, 3)
    ]

    before_odd = move(odd, lambda y, z, c: (y, z + 1, c) if z < Z - 1 else None)
    before_even = move(even, lambda y, z, c: (y, z + 1, c) if z < Z - 1 else None)
    wrapped = move(both, lambda y, z, c: (y + 1, 0, c) if z == Z - 1 else None)
    far = move(odd, lambda y, z, c: (y + 1, z - 6, c) if z >= Z - 2 else None)
    held = jnp.where(y == 0, piece[0], parts[0] + parts[1] + parts[2])
    extra = move(held[:BLOCK], lambda y, z, c: (y, 0, c) if z == 1 else None)
    got = move(held, lambda y, z, c: (y, z + 4, c) if z < 2 else None)
    held = jnp.where(z < 4, held, got)
    held, extra = lax.optimization_barrier((held, extra))
    got = move(held, lambda y, z, c: (y, z + 2, c) if z % 4 < 2 else None)
    held = jnp.where(z % 4 < 2, held, got)
    first = move(before_odd, lambda y, z, c: (y, z + 1, c) if 0 < z < Z - 1 else None)
    other_both = swap(others(flag(core), gate, residual))
    got = move(held, lambda y, z, c: (y, z + 1, c) if z < Z - 1 else None)
    got, wrapped = lax.optimization_barrier((got, wrapped))
    quarter = join(flag(z), held, got, extra)
    groups = [[(a * Z + b) * CORES + c for a in range(Y)] for b in range(Z) for c in range(CORES)]
    taps = lax.all_gather(quarter, "ctx", axis_index_groups=groups)
    kept, sent, sums = mix(
        flag(core),
        flag(z),
        forward,
        back,
        taps,
        far,
        first,
        wrapped,
        before_even,
        before_odd,
        even,
        odd,
        gate,
        residual,
        other_both,
        skip[None, :],
    )
    size = Y * Z * CORES
    groups = [
        [a * size + b * CORES + c for a in range(8) for c in range(CORES)] for b in range(Y * Z)
    ]
    squares = lax.all_to_all(sums, ("ch", "ctx"), 0, 0, axis_index_groups=groups)
    received = swap(sent)
    lead = core == 0
    new_residual = jnp.concatenate(
        [jnp.where(lead, kept, received), jnp.where(lead, received, kept)], axis=1
    )
    scale = lax.rsqrt(jnp.sum(squares[:, 0], axis=0) / D + EPS)[:, None]
    normed = new_residual.astype(jnp.float32) * scale * gain.astype(jnp.float32)[None, :]
    return (new_residual, normed.astype(jnp.bfloat16))


def solution(mesh):
    placed = (P("ctx", "ch"), P("ctx", "ch"), P("ctx", "ch"), P("ch"), P("ctx", "ch"), P("ch"))
    return jax.shard_map(
        local,
        mesh=mesh,
        in_specs=placed,
        out_specs=(P("ctx", "ch"), P("ctx", "ch")),
        check_vma=False,
    )
```
